256 devices in a mesh: path: 64 (over y_lo, x, z), shard: 4 (over y_hi, core).
Axes of the slice: x: 4, y: 4 (y_hi: 2, y_lo: 2; y = y_hi * 2 + y_lo), z: 8, core: 2. Of those that a mesh axis runs over, the one named last changes fastest.
Arguments:
- params: float32 [64, 2, 256, 2048], P('path', None, 'shard'), may hold values from -6 to 6
- grads: bfloat16 [64, 2, 256, 2048], P('path', None, 'shard'), may hold values from -480 to 480
- adam_mean: float32 [64, 2, 256, 2048], P('path', None, 'shard'), may hold values from -1.2 to 1.2
- adam_square: float32 [64, 2, 256, 2048], P('path', None, 'shard'), may hold values from 0.001 to 0.3
- anchor: float32 [28, 256, 2048], P(None, ('shard', 'path')), may hold values from -6 to 6
- momentum: float32 [28, 256, 2048], P(None, ('shard', 'path')), may hold values from -3 to 3
- module_low: int32 [64], replicated, may hold values from 0 to 11
- module_high: int32 [64], replicated, may hold values from 0 to 15
- tok_counts: int32 [64], replicated, may hold values from 1024 to 8191
Outputs:
- new_params: float32 [64, 2, 256, 2048], P('path', None, 'shard')
- new_mean: float32 [64, 2, 256, 2048], P('path', None, 'shard')
- new_square: float32 [64, 2, 256, 2048], P('path', None, 'shard')
- new_anchor: float32 [28, 256, 2048], P(None, ('shard', 'path'))
- new_moment: float32 [28, 256, 2048], P(None, ('shard', 'path'))
The draws below stay inside these ranges and needn't reach their ends.
All inputs are finite; a program needn't handle non-finite values.
Results may differ from the reference program's by a relative error of at most 0.0004.
Values sent between devices are 32-bit elements; how exact they have to be, the bound alone decides.
No kernel may reach another device: no remote copies, remote signals or barrier semaphores. Data moves between devices by JAX's collectives and lax.ppermute only.
A program may use at most 128 MiB of HBM per device.

```python
import math
import jax
import jax.numpy as jnp
from jax import lax

D = 2048
LOW = 12
HIGH = 16
INNER_STEP = 500
MODULES = 28
ROWS = 256
PATHS = 64


def draw_grads(key, part):
    key = jax.random.fold_in(key, 11)
    key_base = jax.random.fold_in(key, 0)
    key_rows = jax.random.fold_in(key, 1)
    key_cols = jax.random.fold_in(key, 2)
    key_small = jax.random.fold_in(key, 4)
    rising = jnp.exp(math.log(3.0) * jnp.arange(ROWS, dtype=jnp.float32) / ROWS).reshape(1, 1, ROWS, 1)
    row_scale = jnp.exp(math.log(4.0) * jax.random.uniform(key_rows, (PATHS, 2, ROWS, 1), jnp.float32))
    col_scale = jnp.exp(math.log(10.0) * jax.random.uniform(key_cols, (PATHS, 2, 1, D), jnp.float32))
    order = jax.random.permutation(key_small, PATHS)
    quiet = order < max(PATHS // 8, 2)
    path_scale = jnp.where(quiet, 0.005, 1.0).astype(jnp.float32).reshape(PATHS, 1, 1, 1)
    base_draw = jax.random.truncated_normal(key_base, -4.0, 4.0, (PATHS, 2, ROWS, D), jnp.float32)
    return (base_draw * rising * row_scale * col_scale * path_scale).astype(jnp.bfloat16)


def module_choice(key, count):
    key_order, key_pick, key_place = jax.random.split(key, 3)
    inner = 1 + jax.random.permutation(key_order, count - 2)
    usable = jnp.concatenate([jnp.array([0, count - 1], jnp.int32), inner[:count - 4].astype(jnp.int32)])
    picks = jax.random.randint(key_pick, (PATHS,), 0, count - 2)
    places = jax.random.permutation(key_place, PATHS)
    picks = picks.at[places[0]].set(0).at[places[1]].set(1)
    return usable[picks].astype(jnp.int32)


def draw_module_low(key, part):
    key = jax.random.fold_in(key, 21)
    return module_choice(key, LOW)


def draw_module_high(key, part):
    key = jax.random.fold_in(key, 37)
    return module_choice(key, HIGH)


def plant(drawn, rng, smallest, largest):
    longest = drawn.shape.index(max(drawn.shape))
    spots = []
    for shift in (0, 1):
        where = [jax.random.randint(jax.random.fold_in(rng, axis), (), 0, length) for axis, length in enumerate(drawn.shape)]
        where[longest] = (where[longest] + shift) % drawn.shape[longest]
        spots.append(tuple(where))
    return drawn.at[spots[0]].set(smallest).at[spots[1]].set(largest)


def levels(own_key, dims, cuts, smallest, high):
    loudness, own = 1.0, jax.random.fold_in(own_key, 6)
    for axis_at, blocks in cuts:
        draws = jnp.exp(jax.random.uniform(jax.random.fold_in(own, axis_at), (blocks,), jnp.float32, smallest / len(cuts), high / len(cuts)))
        loudness = loudness * jnp.repeat(draws, dims[axis_at] // blocks).reshape([-1 if axis == axis_at else 1 for axis in range(len(dims))])
    return loudness


def gaussian(key, extent, scale, most, cuts=(), held_as=jnp.bfloat16):
    values = scale * jax.random.normal(key, extent, jnp.float32)
    if cuts:
        values = values * levels(key, extent, cuts, -0.22, 0.18)
    return jnp.clip(values, -most, most).astype(held_as)


def setup_inputs(seed: int = 0) -> dict:
    arg_keys = jax.random.split(jax.random.key(seed), 10)
    params = gaussian(arg_keys[0], (PATHS, 2, ROWS, D), 1.0, 6.0, ((0, 64), (2, 4)), jnp.float32)
    grads = draw_grads(jax.random.fold_in(arg_keys[9], 71), 0)
    adam_mean = gaussian(arg_keys[2], (PATHS, 2, ROWS, D), 0.2, 1.2, ((0, 64), (2, 4)), jnp.float32)
    adam_square = jnp.clip(jnp.exp(math.log(0.3) - 5.7037825 * jax.random.uniform(arg_keys[3], (PATHS, 2, ROWS, D), jnp.float32) ** levels(arg_keys[3], (PATHS, 2, ROWS, D), ((0, 64), (2, 4)), -0.2, 0.2)), 0.001, 0.3)
    anchor = gaussian(arg_keys[4], (MODULES, ROWS, D), 1.0, 6.0, ((1, 256),), jnp.float32)
    momentum = gaussian(arg_keys[5], (MODULES, ROWS, D), 0.5, 3.0, ((1, 256),), jnp.float32)
    module_low = draw_module_low(jax.random.fold_in(arg_keys[9], 71), 0)
    module_high = draw_module_high(jax.random.fold_in(arg_keys[9], 71), 0)
    tok_counts = plant(jax.random.randint(arg_keys[8], (PATHS,), 1024, 8192), jax.random.fold_in(arg_keys[8], 1), 1024, 8191).astype(jnp.int32)
    return {"params": params, "grads": grads, "adam_mean": adam_mean, "adam_square": adam_square, "anchor": anchor, "momentum": momentum, "module_low": module_low, "module_high": module_high, "tok_counts": tok_counts}


BETA_FIRST = 0.9
BETA_SECOND = 0.95
LEARN_RATE = 0.0004
WEIGHT_DECAY = 0.1
ADAM_EPS = 1e-08
OUTER_RATE = 0.7
OUTER_MOMENTUM = 0.9
CLIP_SHARE = 0.2

def reference(params, grads, adam_mean, adam_square, anchor, momentum, module_low, module_high, tok_counts):
    gradient = grads.astype(jnp.float32)
    squares = lax.optimization_barrier(jnp.sum(gradient * gradient, axis=(1, 2, 3)))
    clip_norm = CLIP_SHARE * math.sqrt(2 * ROWS * D)
    factor = jnp.minimum(1.0, clip_norm / jnp.sqrt(squares + 1e-06))[:, None, None, None]
    clipped = gradient * factor
    new_mean = BETA_FIRST * adam_mean + (1.0 - BETA_FIRST) * clipped
    new_square = BETA_SECOND * adam_square + (1.0 - BETA_SECOND) * clipped * clipped
    first_fix = 1.0 - BETA_FIRST ** INNER_STEP
    second_fix = 1.0 - BETA_SECOND ** INNER_STEP
    update = new_mean / first_fix / (jnp.sqrt(new_square / second_fix) + ADAM_EPS) + WEIGHT_DECAY * params
    stepped = params - LEARN_RATE * update
    module_ids = jnp.stack([module_low, module_high + LOW], axis=1).astype(jnp.int32)
    onehot = (module_ids[None, :, :] == jnp.arange(MODULES, dtype=jnp.int32)[:, None, None]).astype(jnp.float32)
    weights = onehot * tok_counts.astype(jnp.float32)[None, :, None]
    totals = lax.optimization_barrier(jnp.sum(weights, axis=(1, 2)))
    summed = jnp.dot(weights.reshape(MODULES, PATHS * 2), stepped.reshape(PATHS * 2, ROWS * D), precision=lax.Precision.HIGHEST).reshape(MODULES, ROWS, D)
    outer_grad = (totals[:, None, None] * anchor - summed) / jnp.maximum(totals, 1.0)[:, None, None]
    new_moment = OUTER_MOMENTUM * momentum + outer_grad
    new_anchor = anchor - OUTER_RATE * (outer_grad + OUTER_MOMENTUM * new_moment)
    new_params = jnp.take(new_anchor, module_ids, axis=0)
    return (new_params, new_mean, new_square, new_anchor, new_moment)
```

```python
import math

import jax
import jax.numpy as jnp
from jax import lax
from jax.experimental import pallas as pl
from jax.experimental.pallas import tpu as pltpu
from jax.sharding import PartitionSpec as P

LOW = 12
INNER_STEP = 500


BETA_FIRST = 0.9
BETA_SECOND = 0.95
LEARN_RATE = 0.0004
WEIGHT_DECAY = 0.1
ADAM_EPS = 1e-08
OUTER_RATE = 0.7
OUTER_MOMENTUM = 0.9
CLIP_SHARE = 0.2

LANES = 128
FIRST_FIX = 1.0 - BETA_FIRST**INNER_STEP
SECOND_FIX = 1.0 - BETA_SECOND**INNER_STEP


def inner_kernel(scalars, params, grads, mean, square, new_mean, new_square, send):
    factor = scalars[0]
    tokens = scalars[1]
    levels, rows, width = params.shape
    chunks = width // LANES
    for level in range(levels):
        for row in range(0, rows, 16):
            for chunk in range(chunks):
                lanes = slice(chunk * LANES, (chunk + 1) * LANES)
                at = (level, slice(row, row + 16), lanes)
                clipped = grads[at].astype(jnp.float32) * factor
                first = BETA_FIRST * mean[at] + (1.0 - BETA_FIRST) * clipped
                second = BETA_SECOND * square[at] + (1.0 - BETA_SECOND) * clipped * clipped
                new_mean[at] = first
                new_square[at] = second
                fixed = second * (1.0 / SECOND_FIX)
                root = fixed * lax.rsqrt(fixed) + ADAM_EPS
                old = params[at]
                update = first * (1.0 / FIRST_FIX) * pl.reciprocal(root, approx=True) + WEIGHT_DECAY * old
                stepped = old - LEARN_RATE * update
                send[slice(row, row + 16), level * chunks + chunk, :] = stepped * tokens


def outer_kernel(low, high, tokens, received, anchor, momentum, new_anchor, new_moment, send, summed, totals):
    paths = received.shape[0]
    modules, chunks, _ = anchor.shape
    summed[...] = jnp.zeros_like(summed)
    for module in range(modules):
        totals[module] = 0

    def add(path, carry):
        for level in range(2):
            module = low[path] if level == 0 else high[path] + LOW
            summed[module] += received[path, level * chunks : (level + 1) * chunks, :]
            totals[module] += tokens[path]
        return carry

    lax.fori_loop(0, paths, add, 0, unroll=4)
    for module in range(modules):
        total = jnp.full((chunks, LANES), totals[module], jnp.int32).astype(jnp.float32)
        old = anchor[module]
        outer_grad = (total * old - summed[module]) / jnp.maximum(total, 1.0)
        moment = OUTER_MOMENTUM * momentum[module] + outer_grad
        new_moment[module] = moment
        new_anchor[module] = old - OUTER_RATE * (outer_grad + OUTER_MOMENTUM * moment)

    def pick(path, carry):
        for level in range(2):
            module = low[path] if level == 0 else high[path] + LOW
            send[path, level * chunks : (level + 1) * chunks, :] = new_anchor[module]
        return carry

    lax.fori_loop(0, paths, pick, 0, unroll=4)


def place_kernel(received, new_params):
    levels, rows, width = new_params.shape
    chunks = width // LANES
    for level in range(levels):
        for row in range(0, rows, 8):
            for chunk in range(chunks):
                lanes = slice(chunk * LANES, (chunk + 1) * LANES)
                new_params[level, slice(row, row + 8), lanes] = received[slice(row, row + 8), level * chunks + chunk, :]


VMEM = pl.BlockSpec(memory_space=pltpu.VMEM)
SMEM = pl.BlockSpec(memory_space=pltpu.SMEM)


def shards(
    params, grads, adam_mean, adam_square, anchor, momentum, module_low, module_high, tok_counts
):
    _, levels, rows, width = params.shape
    modules = anchor.shape[0]
    paths = module_low.shape[0]
    chunks = width // LANES
    f32 = jnp.float32
    gradient = grads.astype(f32)
    squares = lax.psum(jnp.sum(gradient * gradient), "shard")
    all_rows = rows * lax.axis_size("shard")
    clip_norm = CLIP_SHARE * math.sqrt(2 * all_rows * width)
    factor = jnp.minimum(1.0, clip_norm / jnp.sqrt(squares + 1e-06))
    own_tokens = lax.dynamic_index_in_dim(tok_counts, lax.axis_index("path"), keepdims=False)
    scalars = jnp.stack([factor, own_tokens.astype(f32)])
    local = jax.ShapeDtypeStruct((levels, rows, width), f32)
    wire = jax.ShapeDtypeStruct((rows, levels * chunks, LANES), f32)
    owned = jax.ShapeDtypeStruct((modules, chunks, LANES), f32)
    new_mean, new_square, send = pl.pallas_call(
        inner_kernel,
        out_shape=(local, local, wire),
        in_specs=[SMEM] + [VMEM] * 4,
        out_specs=(VMEM,) * 3,
        compiler_params=pltpu.CompilerParams(vmem_limit_bytes=16 * 1024 * 1024),
        name="inner",
    )(scalars, params[0], grads[0], adam_mean[0], adam_square[0])
    received = lax.all_to_all(send, "path", 0, 0, tiled=True)
    new_anchor, new_moment, send_back = pl.pallas_call(
        outer_kernel,
        out_shape=(owned, owned, jax.ShapeDtypeStruct((paths, levels * chunks, LANES), f32)),
        in_specs=[SMEM] * 3 + [VMEM] * 3,
        out_specs=(VMEM,) * 3,
        scratch_shapes=[pltpu.VMEM((modules, chunks, LANES), f32), pltpu.SMEM((modules,), jnp.int32)],
        compiler_params=pltpu.CompilerParams(vmem_limit_bytes=16 * 1024 * 1024),
        name="outer",
    )(
        module_low, module_high, tok_counts, received,
        anchor.reshape(modules, chunks, LANES), momentum.reshape(modules, chunks, LANES),
    )
    returned = lax.all_to_all(send_back, "path", 0, 0, tiled=True)
    new_params = pl.pallas_call(
        place_kernel,
        out_shape=local,
        in_specs=[VMEM],
        out_specs=VMEM,
        compiler_params=pltpu.CompilerParams(vmem_limit_bytes=16 * 1024 * 1024),
        name="place",
    )(returned)
    return (
        new_params[None], new_mean[None], new_square[None],
        new_anchor.reshape(anchor.shape), new_moment.reshape(anchor.shape),
    )


def solution(mesh):
    return jax.shard_map(
        shards,
        mesh=mesh,
        in_specs=(
            P("path", None, "shard", None),
            P("path", None, "shard", None),
            P("path", None, "shard", None),
            P("path", None, "shard", None),
            P(None, ("shard", "path"), None),
            P(None, ("shard", "path"), None),
            P(),
            P(),
            P(),
        ),
        out_specs=(
            P("path", None, "shard", None),
            P("path", None, "shard", None),
            P("path", None, "shard", None),
            P(None, ("shard", "path"), None),
            P(None, ("shard", "path"), None),
        ),
        check_vma=False,
    )
```

```python
import functools
import math

import jax
import jax.numpy as jnp
from jax import lax
from jax.experimental import pallas as pl
from jax.experimental.pallas import tpu as pltpu
from jax.sharding import PartitionSpec as P

LOW = 12
INNER_STEP = 500


BETA_FIRST = 0.9
BETA_SECOND = 0.95
LEARN_RATE = 0.0004
WEIGHT_DECAY = 0.1
ADAM_EPS = 1e-08
OUTER_RATE = 0.7
OUTER_MOMENTUM = 0.9
CLIP_SHARE = 0.2

LANES = 128
FIRST_FIX = 1.0 - BETA_FIRST**INNER_STEP
SECOND_FIX = 1.0 - BETA_SECOND**INNER_STEP


SPAN = 16


def load(sources, buffers, sems, step):
    level, rows = divmod(step * SPAN, sources[0].shape[1])
    copies = []
    for kind, (source, buffer) in enumerate(zip(sources, buffers)):
        at = (level, slice(rows, rows + SPAN))
        copies.append(pltpu.make_async_copy(source.at[at], buffer.at[at], sems.at[kind, step]))
    return copies


def norm_kernel(grads, partial, buffer, sems):
    levels, rows, width = grads.shape
    steps = levels * rows // SPAN
    copies = [load((grads,), (buffer,), sems, step)[0] for step in range(steps)]
    for copy in copies:
        copy.start()
    sums = [jnp.zeros((8, LANES), jnp.float32) for _ in range(4)]
    for step in range(steps):
        copies[step].wait()
        level, row = divmod(step * SPAN, rows)
        for chunk in range(width // LANES):
            part = buffer[level, row : row + SPAN, chunk * LANES : (chunk + 1) * LANES].astype(jnp.float32)
            for half in range(SPAN // 8):
                piece = part[half * 8 : half * 8 + 8]
                slot = (chunk * 2 + half) % 4
                sums[slot] = sums[slot] + piece * piece
    partial[...] = (sums[0] + sums[1]) + (sums[2] + sums[3])


def inner_kernel(
    clip_norm, near, far, decayed, grads, kept_mean, kept_square, new_mean, new_square, send, mean, square, sems
):
    levels, rows, width = decayed.shape
    chunks = width // LANES
    squares = jnp.sum(jnp.sum(near[...] + far[...], axis=0, keepdims=True), axis=1, keepdims=True)
    factor = jnp.minimum(1.0, clip_norm * lax.rsqrt(squares + 1e-06))
    factor = jnp.broadcast_to(factor, (SPAN, LANES))
    stores = []
    for step in range(levels * rows // SPAN):
        level, row = divmod(step * SPAN, rows)
        here = slice(row, row + SPAN)
        for chunk in range(chunks):
            at = (level, here, slice(chunk * LANES, (chunk + 1) * LANES))
            clipped = grads[at].astype(jnp.float32) * factor
            first = kept_mean[at] + (1.0 - BETA_FIRST) * clipped
            second = kept_square[at] + (1.0 - BETA_SECOND) * clipped * clipped
            mean[at] = first
            square[at] = second
            fixed = second * (1.0 / SECOND_FIX)
            root = fixed * lax.rsqrt(fixed) + ADAM_EPS
            update = first * (LEARN_RATE / FIRST_FIX) * pl.reciprocal(root, approx=True)
            send[here, level * chunks + chunk, :] = decayed[at] - update
        for kind, (source, target) in enumerate(((mean, new_mean), (square, new_square))):
            store = pltpu.make_async_copy(source.at[level, here], target.at[level, here], sems.at[kind, step])
            store.start()
            stores.append(store)
    for store in stores:
        store.wait()


def outer_kernel(
    low, high, tokens, received, anchor, momentum, new_anchor, new_moment, send, totals, *sums
):
    paths = received.shape[0]
    modules, chunks, _ = anchor.shape
    for each in sums:
        each[...] = jnp.zeros_like(each)
    for module in range(modules):
        totals[module] = 0
    lanes = len(sums) // 2

    def add(turn, carry):
        for lane in range(lanes):
            path = turn * lanes + lane
            count = tokens[path]
            weight = jnp.full((chunks, LANES), count, jnp.int32).astype(jnp.float32)
            one, two = low[path], high[path]
            sums[lane][one] += weight * received[path, :chunks, :]
            sums[lanes + lane][two] += weight * received[path, chunks:, :]
            totals[one] += count
            totals[two + LOW] += count
        return carry

    lax.fori_loop(0, paths // lanes, add, 0, unroll=2)
    for module in range(modules):
        total = jnp.full((chunks, LANES), totals[module], jnp.int32).astype(jnp.float32)
        old = anchor[module]
        if module < LOW:
            parts = [sums[lane][module] for lane in range(lanes)]
        else:
            parts = [sums[lanes + lane][module - LOW] for lane in range(lanes)]
        outer_grad = (total * old - sum(parts)) / jnp.maximum(total, 1.0)
        moment = OUTER_MOMENTUM * momentum[module] + outer_grad
        new_moment[module] = moment
        new_anchor[module] = old - OUTER_RATE * (outer_grad + OUTER_MOMENTUM * moment)

    def pick(path, carry):
        send[path, :chunks, :] = new_anchor[low[path]]
        send[path, chunks:, :] = new_anchor[high[path] + LOW]
        return carry

    lax.fori_loop(0, paths, pick, 0, unroll=8)


def place_kernel(received, new_params, placed, sems):
    levels, rows, width = new_params.shape
    chunks = width // LANES
    stores = []
    for step in range(levels * rows // SPAN):
        level, row = divmod(step * SPAN, rows)
        here = slice(row, row + SPAN)
        for chunk in range(chunks):
            lanes = slice(chunk * LANES, (chunk + 1) * LANES)
            placed[level, here, lanes] = received[here, level * chunks + chunk, :]
        store = pltpu.make_async_copy(placed.at[level, here], new_params.at[level, here], sems.at[step])
        store.start()
        stores.append(store)
    for store in stores:
        store.wait()


VMEM = pl.BlockSpec(memory_space=pltpu.VMEM)
SMEM = pl.BlockSpec(memory_space=pltpu.SMEM)
HBM = pl.BlockSpec(memory_space=pltpu.HBM)
ANY = pl.BlockSpec(memory_space=pl.ANY)


def shards(
    params, grads, adam_mean, adam_square, anchor, momentum, module_low, module_high, tok_counts
):
    _, levels, rows, width = params.shape
    modules = anchor.shape[0]
    paths = module_low.shape[0]
    chunks = width // LANES
    f32 = jnp.float32
    steps = levels * rows // SPAN
    grant = pltpu.CompilerParams(vmem_limit_bytes=16 * 1024 * 1024)
    local = jax.ShapeDtypeStruct((levels, rows, width), f32)
    wire = jax.ShapeDtypeStruct((rows, levels * chunks, LANES), f32)
    owned = jax.ShapeDtypeStruct((modules, chunks, LANES), f32)
    held = pltpu.VMEM((levels, rows, width), f32)
    held_grads = pltpu.VMEM((levels, rows, width), grads.dtype)
    partial = pl.pallas_call(
        norm_kernel,
        out_shape=jax.ShapeDtypeStruct((8, LANES), f32),
        in_specs=[HBM],
        out_specs=VMEM,
        scratch_shapes=[held_grads, pltpu.SemaphoreType.DMA((1, steps))],
        compiler_params=grant,
        name="norm",
    )(grads[0])
    shard_count = lax.axis_size("shard")
    near = partial + lax.ppermute(partial, "shard", [(i, i ^ 1) for i in range(shard_count)])
    far = lax.ppermute(near, "shard", [(i, i ^ 2) for i in range(shard_count)])
    clip_norm = CLIP_SHARE * math.sqrt(2 * rows * shard_count * width)
    decayed = params[0] * (1.0 - LEARN_RATE * WEIGHT_DECAY)
    kept_mean = BETA_FIRST * adam_mean[0]
    kept_square = BETA_SECOND * adam_square[0]
    new_mean, new_square, send = pl.pallas_call(
        functools.partial(inner_kernel, clip_norm),
        out_shape=(local, local, wire),
        in_specs=[VMEM] * 6,
        out_specs=(HBM, HBM, VMEM),
        scratch_shapes=[held, held, pltpu.SemaphoreType.DMA((2, steps))],
        compiler_params=grant,
        name="inner",
    )(near, far, decayed, grads[0], kept_mean, kept_square)
    received = lax.all_to_all(send, "path", 0, 0, tiled=True)
    new_anchor, new_moment, send_back = pl.pallas_call(
        outer_kernel,
        out_shape=(owned, owned, jax.ShapeDtypeStruct((paths, levels * chunks, LANES), f32)),
        in_specs=[SMEM] * 3 + [VMEM] * 3,
        out_specs=(VMEM,) * 3,
        scratch_shapes=[pltpu.SMEM((modules,), jnp.int32)]
        + [pltpu.VMEM((LOW, chunks, LANES), f32)] * 4 + [pltpu.VMEM((modules - LOW, chunks, LANES), f32)] * 4,
        compiler_params=grant,
        name="outer",
    )(
        module_low, module_high, tok_counts, received,
        anchor.reshape(modules, chunks, LANES), momentum.reshape(modules, chunks, LANES),
    )
    returned = lax.all_to_all(send_back, "path", 0, 0, tiled=True)
    new_params = pl.pallas_call(
        place_kernel,
        out_shape=local,
        in_specs=[VMEM],
        out_specs=HBM,
        scratch_shapes=[held, pltpu.SemaphoreType.DMA((steps,))],
        compiler_params=grant,
        name="place",
    )(returned)
    return (
        new_params[None], new_mean[None], new_square[None],
        new_anchor.reshape(anchor.shape), new_moment.reshape(anchor.shape),
    )


def solution(mesh):
    return jax.shard_map(
        shards,
        mesh=mesh,
        in_specs=(
            P("path", None, "shard", None),
            P("path", None, "shard", None),
            P("path", None, "shard", None),
            P("path", None, "shard", None),
            P(None, ("shard", "path"), None),
            P(None, ("shard", "path"), None),
            P(),
            P(),
            P(),
        ),
        out_specs=(
            P("path", None, "shard", None),
            P("path", None, "shard", None),
            P("path", None, "shard", None),
            P(None, ("shard", "path"), None),
            P(None, ("shard", "path"), None),
        ),
        check_vma=False,
    )
```

```python
import functools
import math

import jax
import jax.numpy as jnp
from jax import lax
from jax.experimental import pallas as pl
from jax.experimental.pallas import tpu as pltpu
from jax.sharding import PartitionSpec as P

LOW = 12
INNER_STEP = 500


BETA_FIRST = 0.9
BETA_SECOND = 0.95
LEARN_RATE = 0.0004
WEIGHT_DECAY = 0.1
ADAM_EPS = 1e-08
OUTER_RATE = 0.7
OUTER_MOMENTUM = 0.9
CLIP_SHARE = 0.2

LANES = 128
SPAN = 16
LANES_OF_SUMS = 2
FIRST_FIX = 1.0 - BETA_FIRST**INNER_STEP
SECOND_FIX = 1.0 - BETA_SECOND**INNER_STEP

VMEM = pl.BlockSpec(memory_space=pltpu.VMEM)
SMEM = pl.BlockSpec(memory_space=pltpu.SMEM)
HBM = pl.BlockSpec(memory_space=pltpu.HBM)


def tiles(shape):
    levels, rows, width = shape
    for step in range(levels * rows // SPAN):
        level, row = divmod(step * SPAN, rows)
        here = slice(row, row + SPAN)
        yield step, level, here, places(level, here, width)


def places(level, here, width):
    return [(chunk, (level, here, slice(chunk * LANES, (chunk + 1) * LANES))) for chunk in range(width // LANES)]


def norm_kernel(grads, partial, buffer, sems):
    copies = []
    for step, level, here, _ in tiles(grads.shape):
        copies.append(pltpu.make_async_copy(grads.at[level, here], buffer.at[level, here], sems.at[step]))
        copies[-1].start()
    sums = [jnp.zeros((8, LANES), jnp.float32) for _ in range(4)]
    for step, _, _, spots in tiles(grads.shape):
        copies[step].wait()
        for chunk, at in spots:
            part = buffer[at].astype(jnp.float32)
            for half in range(SPAN // 8):
                piece = part[half * 8 : half * 8 + 8]
                slot = (chunk * 2 + half) % 4
                sums[slot] = sums[slot] + piece * piece
    partial[...] = (sums[0] + sums[1]) + (sums[2] + sums[3])


def prepare_kernel(ids, anchor, momentum, scaled, inverse, kept_moment, totals):
    modules, chunks, _ = anchor.shape
    paths = ids.shape[0] // 3
    for module in range(modules):
        totals[module] = 0

    def add(path, carry):
        count = ids[2 * paths + path]
        totals[ids[path]] += count
        totals[ids[paths + path] + LOW] += count
        return carry

    lax.fori_loop(0, paths, add, 0, unroll=8)
    for module in range(modules):
        total = jnp.full((chunks, LANES), totals[module], jnp.int32).astype(jnp.float32)
        scaled[module] = total * anchor[module]
        inverse[module] = 1.0 / jnp.maximum(total, 1.0)
        kept_moment[module] = OUTER_MOMENTUM * momentum[module]


def clip_factor(clip_norm, near, far):
    squares = jnp.sum(jnp.sum(near[...] + far[...], axis=0, keepdims=True), axis=1, keepdims=True)
    factor = jnp.minimum(1.0, clip_norm * lax.rsqrt(squares + 1e-06))
    return jnp.broadcast_to(factor, (SPAN, LANES))


def moments(at, factor, grads, kept_mean, kept_square):
    clipped = grads[at].astype(jnp.float32) * factor
    first = kept_mean[at] + (1.0 - BETA_FIRST) * clipped
    second = kept_square[at] + (1.0 - BETA_SECOND) * clipped * clipped
    return first, second


def stepped(first, second, decayed):
    fixed = second * (1.0 / SECOND_FIX)
    root = fixed * lax.rsqrt(fixed) + ADAM_EPS
    return decayed - first * (LEARN_RATE / FIRST_FIX) * pl.reciprocal(root, approx=True)


def write_moments(step, level, here, mean, square, new_mean, new_square, sems):
    stores = []
    for kind, (source, target) in enumerate(((mean, new_mean), (square, new_square))):
        store = pltpu.make_async_copy(source.at[level, here], target.at[level, here], sems.at[kind, step])
        store.start()
        stores.append(store)
    return stores


def lead_kernel(clip_norm, near, far, decayed, grads, kept_mean, kept_square, send):
    factor = clip_factor(clip_norm, near, far)
    for _, level, here, spots in tiles(decayed.shape):
        for chunk, at in spots:
            first, second = moments(at, factor, grads, kept_mean, kept_square)
            send[here, level * len(spots) + chunk, :] = stepped(first, second, decayed[at])


def moment_kernel(clip_norm, near, far, grads, kept_mean, kept_square, new_mean, new_square, mean, square, sems):
    factor = clip_factor(clip_norm, near, far)
    stores = []
    for step, level, here, spots in tiles(grads.shape):
        for _, at in spots:
            mean[at], square[at] = moments(at, factor, grads, kept_mean, kept_square)
        stores += write_moments(step, level, here, mean, square, new_mean, new_square, sems)
    for store in stores:
        store.wait()


def follow_kernel(
    clip_norm, near, far, decayed, grads, kept_mean, kept_square,
    new_mean, new_square, given, kept, mean, square, sems,
):
    factor = clip_factor(clip_norm, near, far)
    levels, rows, width = decayed.shape
    half = rows // 2
    mine = lax.axis_index("path") // half
    stores = []
    step = 0
    for send, side in ((given, 1 - mine), (kept, mine)):
        for row in range(0, half, SPAN):
            here = pl.ds(pl.multiple_of(side * half + row, SPAN), SPAN)
            for level in range(levels):
                spots = places(level, here, width)
                for chunk, at in spots:
                    first, second = moments(at, factor, grads, kept_mean, kept_square)
                    mean[at] = first
                    square[at] = second
                    send[row : row + SPAN, level * len(spots) + chunk, :] = stepped(first, second, decayed[at])
                stores += write_moments(step, level, here, mean, square, new_mean, new_square, sems)
                step += 1
    for store in stores:
        store.wait()


def outer_kernel(
    ids, received, anchor, scaled, inverse, kept_moment, new_anchor, new_moment, send,
    anchor_held, moment_held, sems, *sums,
):
    paths = ids.shape[0] // 3
    rows = received.shape[0]
    modules, chunks, _ = anchor.shape
    first_side = lax.axis_index("path") // rows if rows < paths else 0
    for each in sums:
        each[...] = jnp.zeros_like(each)
    for path in range(paths):
        lane = path % LANES_OF_SUMS
        weight = jnp.full((chunks, LANES), ids[2 * paths + path], jnp.int32).astype(jnp.float32)
        side, row = divmod(path, rows)
        slot = side ^ first_side
        sums[lane][ids[path]] += weight * received[row, slot, :chunks, :]
        sums[LANES_OF_SUMS + lane][ids[paths + path]] += weight * received[row, slot, chunks:, :]
    for module in range(modules):
        start, place = (0, module) if module < LOW else (LANES_OF_SUMS, module - LOW)
        summed = sum(sums[start + lane][place] for lane in range(LANES_OF_SUMS))
        outer_grad = (scaled[module] - summed) * inverse[module]
        moment = kept_moment[module] + outer_grad
        moment_held[module] = moment
        anchor_held[module] = anchor[module] - OUTER_RATE * (outer_grad + OUTER_MOMENTUM * moment)
    stores = [
        pltpu.make_async_copy(anchor_held, new_anchor, sems.at[0]),
        pltpu.make_async_copy(moment_held, new_moment, sems.at[1]),
    ]
    for store in stores:
        store.start()
    for path in range(paths):
        send[path, :chunks, :] = anchor_held[ids[path]]
        send[path, chunks:, :] = anchor_held[ids[paths + path] + LOW]
    for store in stores:
        store.wait()


def place_kernel(received, new_params, placed, sems):
    stores = []
    for step, level, here, spots in tiles(new_params.shape):
        for chunk, at in spots:
            placed[at] = received[here, level * len(spots) + chunk, :]
        store = pltpu.make_async_copy(placed.at[level, here], new_params.at[level, here], sems.at[step])
        store.start()
        stores.append(store)
    for store in stores:
        store.wait()


def shards(
    params, grads, adam_mean, adam_square, anchor, momentum, module_low, module_high, tok_counts
):
    _, levels, rows, width = params.shape
    modules = anchor.shape[0]
    paths = module_low.shape[0]
    chunks = width // LANES
    steps = levels * rows // SPAN
    f32 = jnp.float32
    grant = pltpu.CompilerParams(vmem_limit_bytes=16 * 1024 * 1024)
    local = jax.ShapeDtypeStruct((levels, rows, width), f32)
    wire = jax.ShapeDtypeStruct((rows, levels * chunks, LANES), f32)
    half_wire = jax.ShapeDtypeStruct((rows // 2, levels * chunks, LANES), f32)
    owned = jax.ShapeDtypeStruct((modules, chunks, LANES), f32)
    held = pltpu.VMEM((levels, rows, width), f32)
    pair_sems = pltpu.SemaphoreType.DMA((2, steps))
    ids = jnp.concatenate([module_low, module_high, tok_counts])

    partial = pl.pallas_call(
        norm_kernel,
        out_shape=jax.ShapeDtypeStruct((8, LANES), f32),
        in_specs=[HBM],
        out_specs=VMEM,
        scratch_shapes=[pltpu.VMEM((levels, rows, width), grads.dtype), pltpu.SemaphoreType.DMA((steps,))],
        compiler_params=grant,
        name="norm",
    )(grads[0])
    shard_count = lax.axis_size("shard")
    near = partial + lax.ppermute(partial, "shard", [(i, i ^ 1) for i in range(shard_count)])
    far = lax.ppermute(near, "shard", [(i, i ^ 2) for i in range(shard_count)])
    clip_norm = CLIP_SHARE * math.sqrt(2 * rows * shard_count * width)

    kept_mean = BETA_FIRST * adam_mean[0]
    kept_square = BETA_SECOND * adam_square[0]
    decayed = params[0] * (1.0 - LEARN_RATE * WEIGHT_DECAY)
    gradient = grads[0]
    staged = (decayed, kept_mean, kept_square)
    old_anchor = anchor.reshape(modules, chunks, LANES)
    prepared = pl.pallas_call(
        prepare_kernel,
        out_shape=(owned,) * 3,
        in_specs=[SMEM] + [VMEM] * 2,
        out_specs=(VMEM,) * 3,
        scratch_shapes=[pltpu.SMEM((modules,), jnp.int32)],
        compiler_params=grant,
        name="prepare",
    )(ids, old_anchor, momentum.reshape(modules, chunks, LANES))
    prepared = lax.optimization_barrier(prepared)

    def update(received):
        new_anchor, new_moment, send_back = pl.pallas_call(
            outer_kernel,
            out_shape=(owned, owned, jax.ShapeDtypeStruct((paths, levels * chunks, LANES), f32)),
            in_specs=[SMEM] + [VMEM] * 5,
            out_specs=(HBM, HBM, VMEM),
            scratch_shapes=[pltpu.VMEM((modules, chunks, LANES), f32)] * 2 + [pltpu.SemaphoreType.DMA((2,))]
            + [pltpu.VMEM((LOW, chunks, LANES), f32)] * LANES_OF_SUMS
            + [pltpu.VMEM((modules - LOW, chunks, LANES), f32)] * LANES_OF_SUMS,
            compiler_params=grant,
            name="outer",
        )(ids, received, old_anchor, *prepared)
        return lax.all_to_all(send_back, "path", 0, 0, tiled=True), new_anchor, new_moment

    def lead():
        send = pl.pallas_call(
            functools.partial(lead_kernel, clip_norm),
            out_shape=wire,
            in_specs=[VMEM] * 6,
            out_specs=VMEM,
            compiler_params=grant,
            name="lead",
        )(near, far, staged[0], gradient, *staged[1:])
        received = lax.all_to_all(send, "path", 0, 0, tiled=True)
        returned, new_anchor, new_moment = update(received.reshape(rows, 1, levels * chunks, LANES))
        first, second, _ = lax.optimization_barrier((*staged[1:], returned))
        new_mean, new_square = pl.pallas_call(
            functools.partial(moment_kernel, clip_norm),
            out_shape=(local, local),
            in_specs=[VMEM] * 5,
            out_specs=(HBM, HBM),
            scratch_shapes=[held, held, pair_sems],
            compiler_params=grant,
            name="moment",
        )(near, far, gradient, first, second)
        return returned, new_mean, new_square, new_anchor, new_moment

    def follow():
        new_mean, new_square, given, kept = pl.pallas_call(
            functools.partial(follow_kernel, clip_norm),
            out_shape=(local, local, half_wire, half_wire),
            in_specs=[VMEM] * 6,
            out_specs=(HBM, HBM, VMEM, VMEM),
            scratch_shapes=[held, held, pair_sems],
            compiler_params=grant,
            name="follow",
        )(near, far, staged[0], gradient, *staged[1:])
        half = paths // 2
        taken = lax.ppermute(given, "path", [(p, (p + half) % paths) for p in range(paths)])
        pair = jnp.stack([kept, taken], axis=1)
        groups = [list(range(half)), list(range(half, paths))]
        received = lax.all_to_all(pair, "path", 0, 0, axis_index_groups=groups, tiled=True)
        returned, new_anchor, new_moment = update(received)
        return returned, new_mean, new_square, new_anchor, new_moment

    leads = lax.rem(lax.axis_index("shard"), 2) == 1
    returned, new_mean, new_square, new_anchor, new_moment = lax.cond(leads, lead, follow)
    new_params = pl.pallas_call(
        place_kernel,
        out_shape=local,
        in_specs=[VMEM],
        out_specs=HBM,
        scratch_shapes=[held, pltpu.SemaphoreType.DMA((steps,))],
        compiler_params=grant,
        name="place",
    )(returned)
    return (
        new_params[None], new_mean[None], new_square[None],
        new_anchor.reshape(anchor.shape), new_moment.reshape(anchor.shape),
    )


def solution(mesh):
    return jax.shard_map(
        shards,
        mesh=mesh,
        in_specs=(
            P("path", None, "shard", None),
            P("path", None, "shard", None),
            P("path", None, "shard", None),
            P("path", None, "shard", None),
            P(None, ("shard", "path"), None),
            P(None, ("shard", "path"), None),
            P(),
            P(),
            P(),
        ),
        out_specs=(
            P("path", None, "shard", None),
            P("path", None, "shard", None),
            P("path", None, "shard", None),
            P(None, ("shard", "path"), None),
            P(None, ("shard", "path"), None),
        ),
        check_vma=False,
    )
```

```python
import functools
import math

import jax
import jax.numpy as jnp
from jax import lax
from jax.experimental import pallas as pl
from jax.experimental.pallas import tpu as pltpu
from jax.sharding import PartitionSpec as P

LOW = 12
INNER_STEP = 500


BETA_FIRST = 0.9
BETA_SECOND = 0.95
LEARN_RATE = 0.0004
WEIGHT_DECAY = 0.1
ADAM_EPS = 1e-08
OUTER_RATE = 0.7
OUTER_MOMENTUM = 0.9
CLIP_SHARE = 0.2

LANES = 128
SPAN = 16
LANES_OF_SUMS = 2
FIRST_FIX = 1.0 - BETA_FIRST**INNER_STEP
SECOND_FIX = 1.0 - BETA_SECOND**INNER_STEP

VMEM = pl.BlockSpec(memory_space=pltpu.VMEM)
SMEM = pl.BlockSpec(memory_space=pltpu.SMEM)
HBM = pl.BlockSpec(memory_space=pltpu.HBM)


def tiles(shape):
    levels, rows, width = shape
    for step in range(levels * rows // SPAN):
        level, row = divmod(step * SPAN, rows)
        here = slice(row, row + SPAN)
        yield step, level, here, places(level, here, width)


def places(level, here, width):
    return [(chunk, (level, here, slice(chunk * LANES, (chunk + 1) * LANES))) for chunk in range(width // LANES)]


def norm_kernel(grads, partial, buffer, sems):
    copies = []
    for step, level, here, _ in tiles(grads.shape):
        copies.append(pltpu.make_async_copy(grads.at[level, here], buffer.at[level, here], sems.at[step]))
        copies[-1].start()
    sums = [jnp.zeros((8, LANES), jnp.float32) for _ in range(4)]
    for step, _, _, spots in tiles(grads.shape):
        copies[step].wait()
        for chunk, at in spots:
            part = buffer[at].astype(jnp.float32)
            for half in range(SPAN // 8):
                piece = part[half * 8 : half * 8 + 8]
                slot = (chunk * 2 + half) % 4
                sums[slot] = sums[slot] + piece * piece
    partial[...] = (sums[0] + sums[1]) + (sums[2] + sums[3])


def prepare_kernel(ids, anchor, momentum, scaled, inverse, kept_moment, totals):
    modules, chunks, _ = anchor.shape
    paths = ids.shape[0] // 3
    for module in range(modules):
        totals[module] = 0

    def add(path, carry):
        count = ids[2 * paths + path]
        totals[ids[path]] += count
        totals[ids[paths + path] + LOW] += count
        return carry

    lax.fori_loop(0, paths, add, 0, unroll=8)
    for module in range(modules):
        total = jnp.full((chunks, LANES), totals[module], jnp.int32).astype(jnp.float32)
        scaled[module] = total * anchor[module]
        inverse[module] = 1.0 / jnp.maximum(total, 1.0)
        kept_moment[module] = OUTER_MOMENTUM * momentum[module]


def clip_factor(clip_norm, near, far):
    squares = jnp.sum(jnp.sum(near[...] + far[...], axis=0, keepdims=True), axis=1, keepdims=True)
    factor = jnp.minimum(1.0, clip_norm * lax.rsqrt(squares + 1e-06))
    return jnp.broadcast_to(factor, (SPAN, LANES))


def moments(at, factor, grads, kept_mean, kept_square):
    clipped = grads[at].astype(jnp.float32) * factor
    first = kept_mean[at] + (1.0 - BETA_FIRST) * clipped
    second = kept_square[at] + (1.0 - BETA_SECOND) * clipped * clipped
    return first, second


def stepped(first, second, decayed):
    fixed = second * (1.0 / SECOND_FIX)
    root = fixed * lax.rsqrt(fixed) + ADAM_EPS
    return decayed - first * (LEARN_RATE / FIRST_FIX) * pl.reciprocal(root, approx=True)


def write_moments(step, level, here, mean, square, new_mean, new_square, sems):
    stores = []
    for kind, (source, target) in enumerate(((mean, new_mean), (square, new_square))):
        store = pltpu.make_async_copy(source.at[level, here], target.at[level, here], sems.at[kind, step])
        store.start()
        stores.append(store)
    return stores


def lead_kernel(clip_norm, near, far, decayed, grads, kept_mean, kept_square, send):
    factor = clip_factor(clip_norm, near, far)
    for _, level, here, spots in tiles(decayed.shape):
        for chunk, at in spots:
            first, second = moments(at, factor, grads, kept_mean, kept_square)
            send[here, level * len(spots) + chunk, :] = stepped(first, second, decayed[at])


def moment_kernel(clip_norm, near, far, grads, kept_mean, kept_square, new_mean, new_square, mean, square, sems):
    factor = clip_factor(clip_norm, near, far)
    stores = []
    for step, level, here, spots in tiles(grads.shape):
        for _, at in spots:
            mean[at], square[at] = moments(at, factor, grads, kept_mean, kept_square)
        stores += write_moments(step, level, here, mean, square, new_mean, new_square, sems)
    for store in stores:
        store.wait()


def follow_kernel(clip_norm, near, far, decayed, grads, kept_mean, kept_square, given, kept):
    factor = clip_factor(clip_norm, near, far)
    levels, rows, width = decayed.shape
    half = rows // 2
    mine = lax.axis_index("path") // half
    for send, side in ((given, 1 - mine), (kept, mine)):
        for row in range(0, half, SPAN):
            here = pl.ds(pl.multiple_of(side * half + row, SPAN), SPAN)
            for level in range(levels):
                spots = places(level, here, width)
                for chunk, at in spots:
                    first, second = moments(at, factor, grads, kept_mean, kept_square)
                    send[row : row + SPAN, level * len(spots) + chunk, :] = stepped(first, second, decayed[at])


def outer_kernel(
    ids, received, anchor, scaled, inverse, kept_moment, new_anchor, new_moment, send,
    anchor_held, moment_held, sems, *sums,
):
    paths = ids.shape[0] // 3
    rows = received.shape[0]
    modules, chunks, _ = anchor.shape
    first_side = lax.axis_index("path") // rows if rows < paths else 0
    for each in sums:
        each[...] = jnp.zeros_like(each)
    for path in range(paths):
        lane = path % LANES_OF_SUMS
        weight = jnp.full((chunks, LANES), ids[2 * paths + path], jnp.int32).astype(jnp.float32)
        side, row = divmod(path, rows)
        slot = side ^ first_side
        sums[lane][ids[path]] += weight * received[row, slot, :chunks, :]
        sums[LANES_OF_SUMS + lane][ids[paths + path]] += weight * received[row, slot, chunks:, :]
    for module in range(modules):
        start, place = (0, module) if module < LOW else (LANES_OF_SUMS, module - LOW)
        summed = sum(sums[start + lane][place] for lane in range(LANES_OF_SUMS))
        outer_grad = (scaled[module] - summed) * inverse[module]
        moment = kept_moment[module] + outer_grad
        moment_held[module] = moment
        anchor_held[module] = anchor[module] - OUTER_RATE * (outer_grad + OUTER_MOMENTUM * moment)
    stores = [
        pltpu.make_async_copy(anchor_held, new_anchor, sems.at[0]),
        pltpu.make_async_copy(moment_held, new_moment, sems.at[1]),
    ]
    for store in stores:
        store.start()
    for path in range(paths):
        send[path, :chunks, :] = anchor_held[ids[path]]
        send[path, chunks:, :] = anchor_held[ids[paths + path] + LOW]
    for store in stores:
        store.wait()


def place_kernel(received, new_params, placed, sems):
    stores = []
    for step, level, here, spots in tiles(new_params.shape):
        for chunk, at in spots:
            placed[at] = received[here, level * len(spots) + chunk, :]
        store = pltpu.make_async_copy(placed.at[level, here], new_params.at[level, here], sems.at[step])
        store.start()
        stores.append(store)
    for store in stores:
        store.wait()


def shards(
    params, grads, adam_mean, adam_square, anchor, momentum, module_low, module_high, tok_counts
):
    _, levels, rows, width = params.shape
    modules = anchor.shape[0]
    paths = module_low.shape[0]
    chunks = width // LANES
    steps = levels * rows // SPAN
    f32 = jnp.float32
    grant = pltpu.CompilerParams(vmem_limit_bytes=16 * 1024 * 1024)
    local = jax.ShapeDtypeStruct((levels, rows, width), f32)
    wire = jax.ShapeDtypeStruct((rows, levels * chunks, LANES), f32)
    half_wire = jax.ShapeDtypeStruct((rows // 2, levels * chunks, LANES), f32)
    owned = jax.ShapeDtypeStruct((modules, chunks, LANES), f32)
    held = pltpu.VMEM((levels, rows, width), f32)
    pair_sems = pltpu.SemaphoreType.DMA((2, steps))
    ids = jnp.concatenate([module_low, module_high, tok_counts])

    partial = pl.pallas_call(
        norm_kernel,
        out_shape=jax.ShapeDtypeStruct((8, LANES), f32),
        in_specs=[HBM],
        out_specs=VMEM,
        scratch_shapes=[pltpu.VMEM((levels, rows, width), grads.dtype), pltpu.SemaphoreType.DMA((steps,))],
        compiler_params=grant,
        name="norm",
    )(grads[0])
    shard_count = lax.axis_size("shard")
    near = partial + lax.ppermute(partial, "shard", [(i, i ^ 1) for i in range(shard_count)])
    clip_norm = CLIP_SHARE * math.sqrt(2 * rows * shard_count * width)

    near, old_params, old_mean, old_square = lax.optimization_barrier((near, params[0], adam_mean[0], adam_square[0]))
    far = lax.ppermute(near, "shard", [(i, i ^ 2) for i in range(shard_count)])
    kept_mean = BETA_FIRST * old_mean
    kept_square = BETA_SECOND * old_square
    decayed = old_params * (1.0 - LEARN_RATE * WEIGHT_DECAY)
    gradient = grads[0]
    staged = (decayed, kept_mean, kept_square)
    old_anchor = anchor.reshape(modules, chunks, LANES)
    prepared = pl.pallas_call(
        prepare_kernel,
        out_shape=(owned,) * 3,
        in_specs=[SMEM] + [VMEM] * 2,
        out_specs=(VMEM,) * 3,
        scratch_shapes=[pltpu.SMEM((modules,), jnp.int32)],
        compiler_params=grant,
        name="prepare",
    )(ids, old_anchor, momentum.reshape(modules, chunks, LANES))
    prepared = lax.optimization_barrier(prepared)

    def update(received):
        new_anchor, new_moment, send_back = pl.pallas_call(
            outer_kernel,
            out_shape=(owned, owned, jax.ShapeDtypeStruct((paths, levels * chunks, LANES), f32)),
            in_specs=[SMEM] + [VMEM] * 5,
            out_specs=(HBM, HBM, VMEM),
            scratch_shapes=[pltpu.VMEM((modules, chunks, LANES), f32)] * 2 + [pltpu.SemaphoreType.DMA((2,))]
            + [pltpu.VMEM((LOW, chunks, LANES), f32)] * LANES_OF_SUMS
            + [pltpu.VMEM((modules - LOW, chunks, LANES), f32)] * LANES_OF_SUMS,
            compiler_params=grant,
            name="outer",
        )(ids, received, old_anchor, *prepared)
        return lax.all_to_all(send_back, "path", 0, 0, tiled=True), new_anchor, new_moment

    def new_moments(first, second):
        return pl.pallas_call(
            functools.partial(moment_kernel, clip_norm),
            out_shape=(local, local),
            in_specs=[VMEM] * 5,
            out_specs=(HBM, HBM),
            scratch_shapes=[held, held, pair_sems],
            compiler_params=grant,
            name="moment",
        )(near, far, gradient, first, second)

    def lead():
        send = pl.pallas_call(
            functools.partial(lead_kernel, clip_norm),
            out_shape=wire,
            in_specs=[VMEM] * 6,
            out_specs=VMEM,
            compiler_params=grant,
            name="lead",
        )(near, far, staged[0], gradient, *staged[1:])
        received = lax.all_to_all(send, "path", 0, 0, tiled=True)
        returned, new_anchor, new_moment = update(received.reshape(rows, 1, levels * chunks, LANES))
        first, second, _ = lax.optimization_barrier((*staged[1:], returned))
        new_mean, new_square = new_moments(first, second)
        return returned, new_mean, new_square, new_anchor, new_moment

    def follow():
        new_mean, new_square = new_moments(*staged[1:])
        first, second, _ = lax.optimization_barrier((*staged[1:], new_mean))
        given, kept = pl.pallas_call(
            functools.partial(follow_kernel, clip_norm),
            out_shape=(half_wire, half_wire),
            in_specs=[VMEM] * 6,
            out_specs=(VMEM, VMEM),
            compiler_params=grant,
            name="follow",
        )(near, far, staged[0], gradient, first, second)
        half = paths // 2
        taken = lax.ppermute(given, "path", [(p, (p + half) % paths) for p in range(paths)])
        pair = jnp.stack([kept, taken], axis=1)
        groups = [list(range(half)), list(range(half, paths))]
        received = lax.all_to_all(pair, "path", 0, 0, axis_index_groups=groups, tiled=True)
        returned, new_anchor, new_moment = update(received)
        return returned, new_mean, new_square, new_anchor, new_moment

    leads = lax.rem(lax.axis_index("shard"), 2) == 1
    returned, new_mean, new_square, new_anchor, new_moment = lax.cond(leads, lead, follow)
    new_params = pl.pallas_call(
        place_kernel,
        out_shape=local,
        in_specs=[VMEM],
        out_specs=HBM,
        scratch_shapes=[held, pltpu.SemaphoreType.DMA((steps,))],
        compiler_params=grant,
        name="place",
    )(returned)
    return (
        new_params[None], new_mean[None], new_square[None],
        new_anchor.reshape(anchor.shape), new_moment.reshape(anchor.shape),
    )


def solution(mesh):
    return jax.shard_map(
        shards,
        mesh=mesh,
        in_specs=(
            P("path", None, "shard", None),
            P("path", None, "shard", None),
            P("path", None, "shard", None),
            P("path", None, "shard", None),
            P(None, ("shard", "path"), None),
            P(None, ("shard", "path"), None),
            P(),
            P(),
            P(),
        ),
        out_specs=(
            P("path", None, "shard", None),
            P("path", None, "shard", None),
            P("path", None, "shard", None),
            P(None, ("shard", "path"), None),
            P(None, ("shard", "path"), None),
        ),
        check_vma=False,
    )
```

```python
import functools
import math

import jax
import jax.numpy as jnp
from jax import lax
from jax.experimental import pallas as pl
from jax.experimental.pallas import tpu as pltpu
from jax.sharding import PartitionSpec as P

LOW = 12
INNER_STEP = 500


BETA_FIRST = 0.9
BETA_SECOND = 0.95
LEARN_RATE = 0.0004
WEIGHT_DECAY = 0.1
ADAM_EPS = 1e-08
OUTER_RATE = 0.7
OUTER_MOMENTUM = 0.9
CLIP_SHARE = 0.2

LANES = 128
SPAN = 16
LANES_OF_SUMS = 2
FIRST_FIX = 1.0 - BETA_FIRST**INNER_STEP
SECOND_FIX = 1.0 - BETA_SECOND**INNER_STEP

VMEM = pl.BlockSpec(memory_space=pltpu.VMEM)
SMEM = pl.BlockSpec(memory_space=pltpu.SMEM)
HBM = pl.BlockSpec(memory_space=pltpu.HBM)


def tiles(shape):
    levels, rows, width = shape
    for step in range(levels * rows // SPAN):
        level, row = divmod(step * SPAN, rows)
        here = slice(row, row + SPAN)
        yield step, level, here, places(level, here, width)


def places(level, here, width):
    return [(chunk, (level, here, slice(chunk * LANES, (chunk + 1) * LANES))) for chunk in range(width // LANES)]


def norm_kernel(grads, partial, buffer, sems):
    copies = []
    for step, level, here, _ in tiles(grads.shape):
        copies.append(pltpu.make_async_copy(grads.at[level, here], buffer.at[level, here], sems.at[step]))
        copies[-1].start()
    sums = [jnp.zeros((8, LANES), jnp.float32) for _ in range(4)]
    for step, _, _, spots in tiles(grads.shape):
        copies[step].wait()
        for chunk, at in spots:
            part = buffer[at].astype(jnp.float32)
            for half in range(SPAN // 8):
                piece = part[half * 8 : half * 8 + 8]
                slot = (chunk * 2 + half) % 4
                sums[slot] = sums[slot] + piece * piece
    partial[...] = (sums[0] + sums[1]) + (sums[2] + sums[3])


def prepare_kernel(ids, anchor, momentum, scaled, inverse, kept_moment, totals):
    modules, chunks, _ = anchor.shape
    paths = ids.shape[0] // 3
    for module in range(modules):
        totals[module] = 0

    def add(path, carry):
        count = ids[2 * paths + path]
        totals[ids[path]] += count
        totals[ids[paths + path] + LOW] += count
        return carry

    lax.fori_loop(0, paths, add, 0, unroll=8)
    for module in range(modules):
        total = jnp.full((chunks, LANES), totals[module], jnp.int32).astype(jnp.float32)
        scaled[module] = total * anchor[module]
        inverse[module] = 1.0 / jnp.maximum(total, 1.0)
        kept_moment[module] = OUTER_MOMENTUM * momentum[module]


def clip_factor(clip_norm, near, far):
    squares = jnp.sum(jnp.sum(near[...] + far[...], axis=0, keepdims=True), axis=1, keepdims=True)
    factor = jnp.minimum(1.0, clip_norm * lax.rsqrt(squares + 1e-06))
    return jnp.broadcast_to(factor, (SPAN, LANES))


def moments(at, factor, grads, kept_mean, kept_square):
    clipped = grads[at].astype(jnp.float32) * factor
    first = kept_mean[at] + (1.0 - BETA_FIRST) * clipped
    second = kept_square[at] + (1.0 - BETA_SECOND) * clipped * clipped
    return first, second


def stepped(first, second, decayed):
    fixed = second * (1.0 / SECOND_FIX)
    root = fixed * lax.rsqrt(fixed) + ADAM_EPS
    return decayed - first * (LEARN_RATE / FIRST_FIX) * pl.reciprocal(root, approx=True)


def write_moments(step, level, here, mean, square, new_mean, new_square, sems):
    stores = []
    for kind, (source, target) in enumerate(((mean, new_mean), (square, new_square))):
        store = pltpu.make_async_copy(source.at[level, here], target.at[level, here], sems.at[kind, step])
        store.start()
        stores.append(store)
    return stores


def lead_kernel(clip_norm, near, far, decayed, grads, kept_mean, kept_square, send):
    factor = clip_factor(clip_norm, near, far)
    for _, level, here, spots in tiles(decayed.shape):
        for chunk, at in spots:
            first, second = moments(at, factor, grads, kept_mean, kept_square)
            send[here, level * len(spots) + chunk, :] = stepped(first, second, decayed[at])


def moment_kernel(clip_norm, near, far, grads, kept_mean, kept_square, new_mean, new_square, mean, square, sems):
    factor = clip_factor(clip_norm, near, far)
    stores = []
    for step, level, here, spots in tiles(grads.shape):
        for _, at in spots:
            mean[at], square[at] = moments(at, factor, grads, kept_mean, kept_square)
        stores += write_moments(step, level, here, mean, square, new_mean, new_square, sems)
    for store in stores:
        store.wait()


def follow_kernel(clip_norm, near, far, decayed, grads, kept_mean, kept_square, given, kept):
    factor = clip_factor(clip_norm, near, far)
    levels, rows, width = decayed.shape
    half = rows // 2
    mine = lax.axis_index("path") // half
    for send, side in ((given, 1 - mine), (kept, mine)):
        for row in range(0, half, SPAN):
            here = pl.ds(pl.multiple_of(side * half + row, SPAN), SPAN)
            for level in range(levels):
                spots = places(level, here, width)
                for chunk, at in spots:
                    first, second = moments(at, factor, grads, kept_mean, kept_square)
                    send[row : row + SPAN, level * len(spots) + chunk, :] = stepped(first, second, decayed[at])


def outer_kernel(
    prepared, ids, received, anchor, *refs,
):
    given, (new_anchor, new_moment, send, anchor_held, moment_held, totals, sems, *sums) = (
        (refs[:3], refs[3:]) if prepared else (refs[:1], refs[1:])
    )
    paths = ids.shape[0] // 3
    rows = received.shape[0]
    modules, chunks, _ = anchor.shape
    first_side = lax.axis_index("path") // rows if rows < paths else 0
    for each in sums:
        each[...] = jnp.zeros_like(each)
    for module in range(0 if prepared else modules):
        totals[module] = 0
    for path in range(paths):
        lane = path % LANES_OF_SUMS
        count = ids[2 * paths + path]
        if not prepared:
            totals[ids[path]] += count
            totals[ids[paths + path] + LOW] += count
        weight = jnp.full((chunks, LANES), count, jnp.int32).astype(jnp.float32)
        side, row = divmod(path, rows)
        slot = side ^ first_side
        sums[lane][ids[path]] += weight * received[row, slot, :chunks, :]
        sums[LANES_OF_SUMS + lane][ids[paths + path]] += weight * received[row, slot, chunks:, :]
    for module in range(modules):
        start, place = (0, module) if module < LOW else (LANES_OF_SUMS, module - LOW)
        summed = sum(sums[start + lane][place] for lane in range(LANES_OF_SUMS))
        if prepared:
            scaled, inverse, kept_moment = (ref[module] for ref in given)
        else:
            total = jnp.full((chunks, LANES), totals[module], jnp.int32).astype(jnp.float32)
            scaled, inverse = total * anchor[module], 1.0 / jnp.maximum(total, 1.0)
            kept_moment = OUTER_MOMENTUM * given[0][module]
        outer_grad = (scaled - summed) * inverse
        moment = kept_moment + outer_grad
        moment_held[module] = moment
        anchor_held[module] = anchor[module] - OUTER_RATE * (outer_grad + OUTER_MOMENTUM * moment)
    stores = [
        pltpu.make_async_copy(anchor_held, new_anchor, sems.at[0]),
        pltpu.make_async_copy(moment_held, new_moment, sems.at[1]),
    ]
    for store in stores:
        store.start()
    for path in range(paths):
        send[path, :chunks, :] = anchor_held[ids[path]]
        send[path, chunks:, :] = anchor_held[ids[paths + path] + LOW]
    for store in stores:
        store.wait()


def place_kernel(received, new_params, placed, sems):
    stores = []
    for step, level, here, spots in tiles(new_params.shape):
        for chunk, at in spots:
            placed[at] = received[here, level * len(spots) + chunk, :]
        store = pltpu.make_async_copy(placed.at[level, here], new_params.at[level, here], sems.at[step])
        store.start()
        stores.append(store)
    for store in stores:
        store.wait()


def shards(
    params, grads, adam_mean, adam_square, anchor, momentum, module_low, module_high, tok_counts
):
    _, levels, rows, width = params.shape
    modules = anchor.shape[0]
    paths = module_low.shape[0]
    chunks = width // LANES
    steps = levels * rows // SPAN
    f32 = jnp.float32
    grant = pltpu.CompilerParams(vmem_limit_bytes=16 * 1024 * 1024)
    local = jax.ShapeDtypeStruct((levels, rows, width), f32)
    wire = jax.ShapeDtypeStruct((rows, levels * chunks, LANES), f32)
    half_wire = jax.ShapeDtypeStruct((rows // 2, levels * chunks, LANES), f32)
    owned = jax.ShapeDtypeStruct((modules, chunks, LANES), f32)
    held = pltpu.VMEM((levels, rows, width), f32)
    pair_sems = pltpu.SemaphoreType.DMA((2, steps))
    ids = jnp.concatenate([module_low, module_high, tok_counts])

    partial = pl.pallas_call(
        norm_kernel,
        out_shape=jax.ShapeDtypeStruct((8, LANES), f32),
        in_specs=[HBM],
        out_specs=VMEM,
        scratch_shapes=[pltpu.VMEM((levels, rows, width), grads.dtype), pltpu.SemaphoreType.DMA((steps,))],
        compiler_params=grant,
        name="norm",
    )(grads[0])
    shard_count = lax.axis_size("shard")
    near = partial + lax.ppermute(partial, "shard", [(i, i ^ 1) for i in range(shard_count)])
    clip_norm = CLIP_SHARE * math.sqrt(2 * rows * shard_count * width)

    near, old_params, old_mean, old_square = lax.optimization_barrier((near, params[0], adam_mean[0], adam_square[0]))
    far = lax.ppermute(near, "shard", [(i, i ^ 2) for i in range(shard_count)])
    kept_mean = BETA_FIRST * old_mean
    kept_square = BETA_SECOND * old_square
    decayed = old_params * (1.0 - LEARN_RATE * WEIGHT_DECAY)
    gradient = grads[0]
    staged = (decayed, kept_mean, kept_square)
    old_anchor = anchor.reshape(modules, chunks, LANES)
    old_momentum = momentum.reshape(modules, chunks, LANES)

    def update(received, prepared, *given):
        new_anchor, new_moment, send_back = pl.pallas_call(
            functools.partial(outer_kernel, prepared),
            out_shape=(owned, owned, jax.ShapeDtypeStruct((paths, levels * chunks, LANES), f32)),
            in_specs=[SMEM] + [VMEM] * (2 + len(given)),
            out_specs=(HBM, HBM, VMEM),
            scratch_shapes=[pltpu.VMEM((modules, chunks, LANES), f32)] * 2
            + [pltpu.SMEM((modules,), jnp.int32), pltpu.SemaphoreType.DMA((2,))]
            + [pltpu.VMEM((LOW, chunks, LANES), f32)] * LANES_OF_SUMS
            + [pltpu.VMEM((modules - LOW, chunks, LANES), f32)] * LANES_OF_SUMS,
            compiler_params=grant,
            name="outer",
        )(ids, received, old_anchor, *given)
        return lax.all_to_all(send_back, "path", 0, 0, tiled=True), new_anchor, new_moment

    def new_moments(first, second):
        return pl.pallas_call(
            functools.partial(moment_kernel, clip_norm),
            out_shape=(local, local),
            in_specs=[VMEM] * 5,
            out_specs=(HBM, HBM),
            scratch_shapes=[held, held, pair_sems],
            compiler_params=grant,
            name="moment",
        )(near, far, gradient, first, second)

    def lead():
        send = pl.pallas_call(
            functools.partial(lead_kernel, clip_norm),
            out_shape=wire,
            in_specs=[VMEM] * 6,
            out_specs=VMEM,
            compiler_params=grant,
            name="lead",
        )(near, far, staged[0], gradient, *staged[1:])
        received = lax.all_to_all(send, "path", 0, 0, tiled=True)
        returned, new_anchor, new_moment = update(
            received.reshape(rows, 1, levels * chunks, LANES), False, old_momentum
        )
        first, second, _ = lax.optimization_barrier((*staged[1:], returned))
        new_mean, new_square = new_moments(first, second)
        return returned, new_mean, new_square, new_anchor, new_moment

    def follow():
        new_mean, new_square = new_moments(*staged[1:])
        first, second, _ = lax.optimization_barrier((*staged[1:], new_mean))
        given, kept = pl.pallas_call(
            functools.partial(follow_kernel, clip_norm),
            out_shape=(half_wire, half_wire),
            in_specs=[VMEM] * 6,
            out_specs=(VMEM, VMEM),
            compiler_params=grant,
            name="follow",
        )(near, far, staged[0], gradient, first, second)
        prepared = pl.pallas_call(
            prepare_kernel,
            out_shape=(owned,) * 3,
            in_specs=[SMEM] + [VMEM] * 2,
            out_specs=(VMEM,) * 3,
            scratch_shapes=[pltpu.SMEM((modules,), jnp.int32)],
            compiler_params=grant,
            name="prepare",
        )(*lax.optimization_barrier((ids, old_anchor, old_momentum, given))[:3])
        half = paths // 2
        taken = lax.ppermute(given, "path", [(p, (p + half) % paths) for p in range(paths)])
        taken, prepared = lax.optimization_barrier((taken, prepared))
        pair = jnp.stack([kept, taken], axis=1)
        groups = [list(range(half)), list(range(half, paths))]
        received = lax.all_to_all(pair, "path", 0, 0, axis_index_groups=groups, tiled=True)
        returned, new_anchor, new_moment = update(received, True, *prepared)
        return returned, new_mean, new_square, new_anchor, new_moment

    leads = lax.rem(lax.axis_index("shard"), 2) == 1
    returned, new_mean, new_square, new_anchor, new_moment = lax.cond(leads, lead, follow)
    new_params = pl.pallas_call(
        place_kernel,
        out_shape=local,
        in_specs=[VMEM],
        out_specs=HBM,
        scratch_shapes=[held, pltpu.SemaphoreType.DMA((steps,))],
        compiler_params=grant,
        name="place",
    )(returned)
    return (
        new_params[None], new_mean[None], new_square[None],
        new_anchor.reshape(anchor.shape), new_moment.reshape(anchor.shape),
    )


def solution(mesh):
    return jax.shard_map(
        shards,
        mesh=mesh,
        in_specs=(
            P("path", None, "shard", None),
            P("path", None, "shard", None),
            P("path", None, "shard", None),
            P("path", None, "shard", None),
            P(None, ("shard", "path"), None),
            P(None, ("shard", "path"), None),
            P(),
            P(),
            P(),
        ),
        out_specs=(
            P("path", None, "shard", None),
            P("path", None, "shard", None),
            P("path", None, "shard", None),
            P(None, ("shard", "path"), None),
            P(None, ("shard", "path"), None),
        ),
        check_vma=False,
    )
```

```python
import functools
import math

import jax
import jax.numpy as jnp
from jax import lax
from jax.experimental import pallas as pl
from jax.experimental.pallas import tpu as pltpu
from jax.sharding import PartitionSpec as P

LOW = 12
INNER_STEP = 500


BETA_FIRST = 0.9
BETA_SECOND = 0.95
LEARN_RATE = 0.0004
WEIGHT_DECAY = 0.1
ADAM_EPS = 1e-08
OUTER_RATE = 0.7
OUTER_MOMENTUM = 0.9
CLIP_SHARE = 0.2

LANES = 128
SPAN = 16
LANES_OF_SUMS = 2
FIRST_FIX = 1.0 - BETA_FIRST**INNER_STEP
SECOND_FIX = 1.0 - BETA_SECOND**INNER_STEP

VMEM = pl.BlockSpec(memory_space=pltpu.VMEM)
SMEM = pl.BlockSpec(memory_space=pltpu.SMEM)
HBM = pl.BlockSpec(memory_space=pltpu.HBM)


def tiles(shape):
    levels, rows, width = shape
    for step in range(levels * rows // SPAN):
        level, row = divmod(step * SPAN, rows)
        here = slice(row, row + SPAN)
        yield step, level, here, places(level, here, width)


def places(level, here, width):
    return [(chunk, (level, here, slice(chunk * LANES, (chunk + 1) * LANES))) for chunk in range(width // LANES)]


def norm_kernel(grads, partial, buffer, sems):
    copies = []
    for step, level, here, _ in tiles(grads.shape):
        copies.append(pltpu.make_async_copy(grads.at[level, here], buffer.at[level, here], sems.at[step]))
        copies[-1].start()
    sums = [jnp.zeros((8, LANES), jnp.float32) for _ in range(4)]
    for step, _, _, spots in tiles(grads.shape):
        copies[step].wait()
        for chunk, at in spots:
            part = buffer[at].astype(jnp.float32)
            for half in range(SPAN // 8):
                piece = part[half * 8 : half * 8 + 8]
                slot = (chunk * 2 + half) % 4
                sums[slot] = sums[slot] + piece * piece
    partial[...] = (sums[0] + sums[1]) + (sums[2] + sums[3])


def prepare_kernel(ids, anchor, momentum, scaled, inverse, kept_moment, totals):
    modules, chunks, _ = anchor.shape
    paths = ids.shape[0] // 3
    for module in range(modules):
        totals[module] = 0

    def add(path, carry):
        count = ids[2 * paths + path]
        totals[ids[path]] += count
        totals[ids[paths + path] + LOW] += count
        return carry

    lax.fori_loop(0, paths, add, 0, unroll=8)
    for module in range(modules):
        total = jnp.full((chunks, LANES), totals[module], jnp.int32).astype(jnp.float32)
        scaled[module] = total * anchor[module]
        inverse[module] = 1.0 / jnp.maximum(total, 1.0)
        kept_moment[module] = OUTER_MOMENTUM * momentum[module]


def clip_factor(clip_norm, near, far):
    squares = jnp.sum(jnp.sum(near[...] + far[...], axis=0, keepdims=True), axis=1, keepdims=True)
    factor = jnp.minimum(1.0, clip_norm * lax.rsqrt(squares + 1e-06))
    return jnp.broadcast_to(factor, (SPAN, LANES))


def moments(at, factor, grads, kept_mean, kept_square):
    clipped = grads[at].astype(jnp.float32) * factor
    first = kept_mean[at] + (1.0 - BETA_FIRST) * clipped
    second = kept_square[at] + (1.0 - BETA_SECOND) * clipped * clipped
    return first, second


def stepped(first, second, decayed):
    fixed = second * (1.0 / SECOND_FIX)
    root = fixed * lax.rsqrt(fixed) + ADAM_EPS
    return decayed - first * (LEARN_RATE / FIRST_FIX) * pl.reciprocal(root, approx=True)


def write_moments(step, level, here, mean, square, new_mean, new_square, sems):
    stores = []
    for kind, (source, target) in enumerate(((mean, new_mean), (square, new_square))):
        store = pltpu.make_async_copy(source.at[level, here], target.at[level, here], sems.at[kind, step])
        store.start()
        stores.append(store)
    return stores


def lead_kernel(clip_norm, near, far, decayed, grads, kept_mean, kept_square, send):
    factor = clip_factor(clip_norm, near, far)
    for _, level, here, spots in tiles(decayed.shape):
        for chunk, at in spots:
            first, second = moments(at, factor, grads, kept_mean, kept_square)
            send[here, level * len(spots) + chunk, :] = stepped(first, second, decayed[at])


def moment_kernel(clip_norm, near, far, grads, kept_mean, kept_square, new_mean, new_square, mean, square, sems):
    factor = clip_factor(clip_norm, near, far)
    stores = []
    for step, level, here, spots in tiles(grads.shape):
        for _, at in spots:
            mean[at], square[at] = moments(at, factor, grads, kept_mean, kept_square)
        stores += write_moments(step, level, here, mean, square, new_mean, new_square, sems)
    for store in stores:
        store.wait()


def follow_kernel(clip_norm, near, far, decayed, grads, kept_mean, kept_square, given, kept):
    factor = clip_factor(clip_norm, near, far)
    levels, rows, width = decayed.shape
    half = rows // 2
    mine = lax.axis_index("path") // half
    for send, side in ((given, 1 - mine), (kept, mine)):
        for row in range(0, half, SPAN):
            here = pl.ds(pl.multiple_of(side * half + row, SPAN), SPAN)
            for level in range(levels):
                spots = places(level, here, width)
                for chunk, at in spots:
                    first, second = moments(at, factor, grads, kept_mean, kept_square)
                    send[row : row + SPAN, level * len(spots) + chunk, :] = stepped(first, second, decayed[at])


def outer_kernel(
    prepared, ids, received, anchor, *refs,
):
    given, (new_anchor, new_moment, send, anchor_held, moment_held, totals, sems, *sums) = (
        (refs[:3], refs[3:]) if prepared else (refs[:1], refs[1:])
    )
    paths = ids.shape[0] // 3
    rows = received.shape[0]
    modules, chunks, _ = anchor.shape
    first_side = lax.axis_index("path") // rows if rows < paths else 0
    for each in sums:
        each[...] = jnp.zeros_like(each)
    for module in range(0 if prepared else modules):
        totals[module] = 0
    for path in range(paths):
        lane = path % LANES_OF_SUMS
        count = ids[2 * paths + path]
        if not prepared:
            totals[ids[path]] += count
            totals[ids[paths + path] + LOW] += count
        weight = jnp.full((chunks, LANES), count, jnp.int32).astype(jnp.float32)
        side, row = divmod(path, rows)
        slot = side ^ first_side
        sums[lane][ids[path]] += weight * received[row, slot, :chunks, :]
        sums[LANES_OF_SUMS + lane][ids[paths + path]] += weight * received[row, slot, chunks:, :]
    for module in range(modules):
        start, place = (0, module) if module < LOW else (LANES_OF_SUMS, module - LOW)
        summed = sum(sums[start + lane][place] for lane in range(LANES_OF_SUMS))
        if prepared:
            scaled, inverse, kept_moment = (ref[module] for ref in given)
        else:
            total = jnp.full((chunks, LANES), totals[module], jnp.int32).astype(jnp.float32)
            scaled, inverse = total * anchor[module], 1.0 / jnp.maximum(total, 1.0)
            kept_moment = OUTER_MOMENTUM * given[0][module]
        outer_grad = (scaled - summed) * inverse
        moment = kept_moment + outer_grad
        moment_held[module] = moment
        anchor_held[module] = anchor[module] - OUTER_RATE * (outer_grad + OUTER_MOMENTUM * moment)
    stores = [
        pltpu.make_async_copy(anchor_held, new_anchor, sems.at[0]),
        pltpu.make_async_copy(moment_held, new_moment, sems.at[1]),
    ]
    for store in stores:
        store.start()
    for path in range(paths):
        send[path, :chunks, :] = anchor_held[ids[path]]
        send[path, chunks:, :] = anchor_held[ids[paths + path] + LOW]
    for store in stores:
        store.wait()


def place_kernel(received, new_params, placed, sems):
    stores = []
    for step, level, here, spots in tiles(new_params.shape):
        for chunk, at in spots:
            placed[at] = received[here, level * len(spots) + chunk, :]
        store = pltpu.make_async_copy(placed.at[level, here], new_params.at[level, here], sems.at[step])
        store.start()
        stores.append(store)
    for store in stores:
        store.wait()


def shards(
    params, grads, adam_mean, adam_square, anchor, momentum, module_low, module_high, tok_counts
):
    _, levels, rows, width = params.shape
    modules = anchor.shape[0]
    paths = module_low.shape[0]
    chunks = width // LANES
    steps = levels * rows // SPAN
    f32 = jnp.float32
    grant = pltpu.CompilerParams(vmem_limit_bytes=16 * 1024 * 1024)
    local = jax.ShapeDtypeStruct((levels, rows, width), f32)
    wire = jax.ShapeDtypeStruct((rows, levels * chunks, LANES), f32)
    half_wire = jax.ShapeDtypeStruct((rows // 2, levels * chunks, LANES), f32)
    owned = jax.ShapeDtypeStruct((modules, chunks, LANES), f32)
    held = pltpu.VMEM((levels, rows, width), f32)
    pair_sems = pltpu.SemaphoreType.DMA((2, steps))
    ids = jnp.concatenate([module_low, module_high, tok_counts])

    partial = pl.pallas_call(
        norm_kernel,
        out_shape=jax.ShapeDtypeStruct((8, LANES), f32),
        in_specs=[HBM],
        out_specs=VMEM,
        scratch_shapes=[pltpu.VMEM((levels, rows, width), grads.dtype), pltpu.SemaphoreType.DMA((steps,))],
        compiler_params=grant,
        name="norm",
    )(grads[0])
    shard_count = lax.axis_size("shard")
    near = partial + lax.ppermute(partial, "shard", [(i, i ^ 1) for i in range(shard_count)])
    clip_norm = CLIP_SHARE * math.sqrt(2 * rows * shard_count * width)

    near, old_mean, old_square = lax.optimization_barrier((near, adam_mean[0], adam_square[0]))
    far = lax.ppermute(near, "shard", [(i, i ^ 2) for i in range(shard_count)])
    kept_mean = BETA_FIRST * old_mean
    kept_square = BETA_SECOND * old_square
    decayed = params[0] * (1.0 - LEARN_RATE * WEIGHT_DECAY)
    gradient = grads[0]
    staged = (decayed, kept_mean, kept_square)
    old_anchor = anchor.reshape(modules, chunks, LANES)
    old_momentum = momentum.reshape(modules, chunks, LANES)

    def update(received, prepared, *given):
        new_anchor, new_moment, send_back = pl.pallas_call(
            functools.partial(outer_kernel, prepared),
            out_shape=(owned, owned, jax.ShapeDtypeStruct((paths, levels * chunks, LANES), f32)),
            in_specs=[SMEM] + [VMEM] * (2 + len(given)),
            out_specs=(HBM, HBM, VMEM),
            scratch_shapes=[pltpu.VMEM((modules, chunks, LANES), f32)] * 2
            + [pltpu.SMEM((modules,), jnp.int32), pltpu.SemaphoreType.DMA((2,))]
            + [pltpu.VMEM((LOW, chunks, LANES), f32)] * LANES_OF_SUMS
            + [pltpu.VMEM((modules - LOW, chunks, LANES), f32)] * LANES_OF_SUMS,
            compiler_params=grant,
            name="outer",
        )(ids, received, old_anchor, *given)
        return lax.all_to_all(send_back, "path", 0, 0, tiled=True), new_anchor, new_moment

    def new_moments(first, second):
        return pl.pallas_call(
            functools.partial(moment_kernel, clip_norm),
            out_shape=(local, local),
            in_specs=[VMEM] * 5,
            out_specs=(HBM, HBM),
            scratch_shapes=[held, held, pair_sems],
            compiler_params=grant,
            name="moment",
        )(near, far, gradient, first, second)

    def lead():
        send = pl.pallas_call(
            functools.partial(lead_kernel, clip_norm),
            out_shape=wire,
            in_specs=[VMEM] * 6,
            out_specs=VMEM,
            compiler_params=grant,
            name="lead",
        )(near, far, staged[0], gradient, *staged[1:])
        received = lax.all_to_all(send, "path", 0, 0, tiled=True)
        returned, new_anchor, new_moment = update(
            received.reshape(rows, 1, levels * chunks, LANES), False, old_momentum
        )
        first, second, _ = lax.optimization_barrier((*staged[1:], returned))
        new_mean, new_square = new_moments(first, second)
        return returned, new_mean, new_square, new_anchor, new_moment

    def follow():
        new_mean, new_square = new_moments(*staged[1:])
        first, second, _ = lax.optimization_barrier((*staged[1:], new_mean))
        given, kept = pl.pallas_call(
            functools.partial(follow_kernel, clip_norm),
            out_shape=(half_wire, half_wire),
            in_specs=[VMEM] * 6,
            out_specs=(VMEM, VMEM),
            compiler_params=grant,
            name="follow",
        )(near, far, staged[0], gradient, first, second)
        prepared = pl.pallas_call(
            prepare_kernel,
            out_shape=(owned,) * 3,
            in_specs=[SMEM] + [VMEM] * 2,
            out_specs=(VMEM,) * 3,
            scratch_shapes=[pltpu.SMEM((modules,), jnp.int32)],
            compiler_params=grant,
            name="prepare",
        )(*lax.optimization_barrier((ids, old_anchor, old_momentum, given))[:3])
        half = paths // 2
        taken = lax.ppermute(given, "path", [(p, (p + half) % paths) for p in range(paths)])
        taken, prepared = lax.optimization_barrier((taken, prepared))
        pair = jnp.stack([kept, taken], axis=1)
        groups = [list(range(half)), list(range(half, paths))]
        received = lax.all_to_all(pair, "path", 0, 0, axis_index_groups=groups, tiled=True)
        returned, new_anchor, new_moment = update(received, True, *prepared)
        return returned, new_mean, new_square, new_anchor, new_moment

    leads = lax.rem(lax.axis_index("shard"), 2) == 1
    returned, new_mean, new_square, new_anchor, new_moment = lax.cond(leads, lead, follow)
    new_params = pl.pallas_call(
        place_kernel,
        out_shape=local,
        in_specs=[VMEM],
        out_specs=HBM,
        scratch_shapes=[held, pltpu.SemaphoreType.DMA((steps,))],
        compiler_params=grant,
        name="place",
    )(returned)
    return (
        new_params[None], new_mean[None], new_square[None],
        new_anchor.reshape(anchor.shape), new_moment.reshape(anchor.shape),
    )


def solution(mesh):
    return jax.shard_map(
        shards,
        mesh=mesh,
        in_specs=(
            P("path", None, "shard", None),
            P("path", None, "shard", None),
            P("path", None, "shard", None),
            P("path", None, "shard", None),
            P(None, ("shard", "path"), None),
            P(None, ("shard", "path"), None),
            P(),
            P(),
            P(),
        ),
        out_specs=(
            P("path", None, "shard", None),
            P("path", None, "shard", None),
            P("path", None, "shard", None),
            P(None, ("shard", "path"), None),
            P(None, ("shard", "path"), None),
        ),
        check_vma=False,
    )
```
